32 devices in a mesh: dp: 16 (over z, y, core), tensor: 2 (over x).
Axes of the slice: x: 2, y: 2, z: 4, core: 2. Of those that a mesh axis runs over, the one named last changes fastest.
Arguments:
- queries: bfloat16 [8192, 2048], P('dp', 'tensor'), may hold values from -360 to 360
- neighbours: int32 [128, 2], P('dp'), may hold values from 0 to 15, as said below
- counts: int32 [128], P('dp'), may hold values from 1 to 2
- states: bfloat16 [16, 128, 4096], P('dp'), may hold values from -6 to 6
- w_key: bfloat16 [4096, 2048], P('dp', 'tensor'), may hold values from -0.09375 to 0.09375
- w_value: bfloat16 [4096, 2048], P('dp', 'tensor'), may hold values from -0.09375 to 0.09375
- cotangent: bfloat16 [8192, 2048], P('dp', 'tensor'), may hold values from -6 to 6
Outputs:
- context: bfloat16 [8192, 2048], P('dp', 'tensor')
- query_grad: bfloat16 [8192, 2048], P('dp', 'tensor')
- state_grad: bfloat16 [16, 128, 4096], P('dp', None, 'tensor')
The draws below stay inside these ranges and needn't reach their ends.
Inputs may be any that keep to these rules, and one draw needn't show every extreme that they name: Neighbour n is held by dp index n. Among the 16 slots of one index of dp, at most 1 name neighbours of one holder, and some holder is named exactly 1 times.
All inputs are finite; a program needn't handle non-finite values.
Results may differ from the reference program's by a relative error of at most 0.035.
The reference program's roundings to bfloat16 on the way count: a program that leaves them out, or rounds other values in their place, can miss the bound.
Values may be sent and summed in bfloat16 or wider, within the bound.
No kernel may reach another device: no remote copies, remote signals or barrier semaphores. Data moves between devices by JAX's collectives and lax.ppermute only.
A program may use at most 128 MiB of HBM per device.

```python
import math
import jax
import jax.numpy as jnp
from jax import lax

D = 4096
HEADS = 16
HEAD = 128
CQ = 64
NL = 128
NEIGH = 2
SPANS = 8
NBR_DEV = 1
OWNERS = 16
NBRS = 16
NCHUNKS = 128
TOKENS = 8192
N_DP = 16
N_TENSOR = 2


def draw_neighbours(key, part):
    key_hot, key_noise, key_local = jax.random.split(key, 3)
    hot_level = jax.random.randint(key_hot, (OWNERS,), 0, 64)
    noise_level = jax.random.randint(key_noise, (OWNERS, OWNERS), 0, 64)
    priority = (hot_level[None, :] + noise_level) * OWNERS + jnp.arange(OWNERS, dtype=jnp.int32)[None, :]
    ranking = jnp.argsort(-priority, axis=1, stable=True).astype(jnp.int32)
    slot_pos = jnp.arange(SPANS * NEIGH, dtype=jnp.int32) % OWNERS
    holder = ranking[:, slot_pos]
    local_index = jax.random.randint(key_local, (OWNERS, SPANS * NEIGH), 0, NBR_DEV)
    return (holder * NBR_DEV + local_index).reshape(OWNERS * SPANS, NEIGH).astype(jnp.int32)


def draw_queries(key, part):
    key_base = jax.random.fold_in(key, 0)
    base = jax.random.truncated_normal(key_base, -6.0, 6.0, (TOKENS, HEADS * HEAD), jnp.float32)
    return base.astype(jnp.bfloat16)


def set_ends(values, rng, smallest, largest):
    extent = values.shape
    place = [jax.random.randint(jax.random.fold_in(rng, axis), (), 0, extent[axis]) for axis in range(len(extent))]
    values = values.at[tuple(place)].set(smallest)
    longest = extent.index(max(extent))
    place[longest] = (place[longest] + 1) % extent[longest]
    return values.at[tuple(place)].set(largest)


def levels(rng, shape, cuts, low, top_value):
    level = 1.0
    for dim, blocks in cuts:
        heights = jax.random.uniform(jax.random.fold_in(jax.random.fold_in(rng, 6), dim), (blocks,), jnp.float32, low / len(cuts), top_value / len(cuts))
        level = level * jnp.repeat(jnp.exp(heights), shape[dim] // blocks).reshape((-1,) + (1,) * (len(shape) - 1 - dim))
    return level


def scatter_about(own_key, dims, width, most, pieces=(), held_as=jnp.bfloat16):
    values = jax.random.normal(own_key, dims, jnp.float32) * width
    if len(pieces) > 0:
        values = levels(own_key, dims, pieces, -0.22, 0.18) * values
    return jnp.clip(values, min=-most, max=most).astype(held_as)


def setup_inputs(seed: int = 0) -> dict:
    arg_keys = jax.random.split(jax.random.key(seed), 8)
    queries = draw_queries(jax.random.fold_in(arg_keys[7], 71), 0)
    neighbours = draw_neighbours(jax.random.fold_in(arg_keys[7], 71), 0)
    counts = set_ends(jax.random.randint(arg_keys[2], (NCHUNKS,), 1, NEIGH + 1), jax.random.fold_in(arg_keys[2], 1), 1, NEIGH).astype(jnp.int32)
    states = scatter_about(arg_keys[3], (NBRS, NL, D), 1.0, 6.0, ((0, 16),))
    w_key = scatter_about(arg_keys[4], (D, HEADS * HEAD), D ** -0.5, 0.09375, ((0, 16), (1, 2)))
    w_value = scatter_about(arg_keys[5], (D, HEADS * HEAD), D ** -0.5, 0.09375, ((0, 16), (1, 2)))
    cotangent = scatter_about(arg_keys[6], (TOKENS, HEADS * HEAD), 1.0, 6.0, ((0, 16), (1, 2)))
    return dict(queries=queries, neighbours=neighbours, counts=counts, states=states, w_key=w_key, w_value=w_value, cotangent=cotangent)


def rounded(x):
    return lax.optimization_barrier(x.astype(jnp.bfloat16)).astype(jnp.float32)

def reference(queries, neighbours, counts, states, w_key, w_value, cotangent):
    score_scale = 1.0 / math.sqrt(HEAD)
    flat_states = states.reshape(NBRS * NL, D)
    key_rows = jnp.dot(flat_states, w_key, preferred_element_type=jnp.float32).astype(jnp.bfloat16).reshape(NBRS, NL, HEADS, HEAD)
    value_rows = jnp.dot(flat_states, w_value, preferred_element_type=jnp.float32).astype(jnp.bfloat16).reshape(NBRS, NL, HEADS, HEAD)
    inputs = (queries.reshape(N_DP, SPANS, CQ, HEADS, HEAD), cotangent.reshape(N_DP, SPANS, CQ, HEADS, HEAD), neighbours.reshape(N_DP, SPANS, NEIGH).astype(jnp.int32), counts.reshape(N_DP, SPANS).astype(jnp.int32))

    def one_block(carried, block_in):
        key_acc, value_acc = carried
        query_blk, grad_blk, id_blk, count_blk = block_in
        key_sel = key_rows[id_blk].astype(jnp.float32)
        value_sel = value_rows[id_blk].astype(jnp.float32)
        query_f = query_blk.astype(jnp.float32)
        scores = jnp.einsum('cqhd,cjkhd->cjhqk', query_f, key_sel) * score_scale
        row_max = lax.optimization_barrier(jnp.max(scores, axis=-1, keepdims=True))
        log_total = row_max[..., 0] + jnp.log(lax.optimization_barrier(jnp.sum(jnp.exp(scores - row_max), axis=-1)))
        prob_rows = jnp.exp(scores - log_total[..., None])
        prob_half = rounded(prob_rows)
        partial_value = rounded(jnp.einsum('cjhqk,cjkhd->cjqhd', prob_half, value_sel))
        log_part = jnp.transpose(log_total, (0, 1, 3, 2))
        is_valid = jnp.arange(NEIGH, dtype=jnp.int32)[None, :] < count_blk[:, None]
        live = is_valid[:, :, None, None]
        masked = jnp.where(live, log_part, -1e+30)
        top_part = lax.optimization_barrier(jnp.max(masked, axis=1, keepdims=True))
        raw_weight = jnp.where(live, jnp.exp(masked - top_part), 0.0)
        mix_weight = raw_weight / lax.optimization_barrier(jnp.sum(raw_weight, axis=1, keepdims=True))
        mixed_rows = lax.optimization_barrier(jnp.sum(mix_weight[..., None] * partial_value, axis=1))
        grad_rows = grad_blk.astype(jnp.float32)
        part_grad = rounded(mix_weight[..., None] * grad_rows[:, None])
        lse_grad = mix_weight * lax.optimization_barrier(jnp.sum(grad_rows[:, None] * (partial_value - mixed_rows[:, None]), axis=-1))
        rest_term = lax.optimization_barrier(jnp.sum(part_grad * partial_value, axis=-1)) - lse_grad
        dprob = jnp.einsum('cjqhd,cjkhd->cjhqk', part_grad, value_sel)
        dscore = prob_rows * (dprob - jnp.transpose(rest_term, (0, 1, 3, 2))[..., None])
        dscore_half = rounded(dscore)
        slot_dq = rounded(jnp.einsum('cjhqk,cjkhd->cjqhd', dscore_half, key_sel) * score_scale)
        query_grad = lax.optimization_barrier(jnp.sum(slot_dq, axis=1)).astype(jnp.bfloat16)
        slot_dk = jnp.einsum('cjhqk,cqhd->cjkhd', dscore_half, query_f) * score_scale
        slot_dv = jnp.einsum('cjhqk,cjqhd->cjkhd', prob_half, part_grad)
        flat_ids = id_blk.reshape(SPANS * NEIGH)
        key_acc = key_acc.at[flat_ids].add(slot_dk.reshape(SPANS * NEIGH, NL, HEADS, HEAD))
        value_acc = value_acc.at[flat_ids].add(slot_dv.reshape(SPANS * NEIGH, NL, HEADS, HEAD))
        return ((key_acc, value_acc), (mixed_rows.astype(jnp.bfloat16), query_grad))
    start_acc = jnp.zeros((NBRS, NL, HEADS, HEAD), jnp.float32)
    (key_acc, value_acc), (context, query_grad) = lax.scan(one_block, (start_acc, start_acc), inputs)
    key_grad = key_acc.astype(jnp.bfloat16).reshape(NBRS * NL, HEADS * HEAD)
    value_grad = value_acc.astype(jnp.bfloat16).reshape(NBRS * NL, HEADS * HEAD)
    group_width = HEADS * HEAD // N_TENSOR
    total_sum = jnp.zeros((NBRS * NL, D), jnp.float32)
    for group in range(N_TENSOR):
        first_col = group * group_width
        term = jnp.dot(key_grad[:, first_col:first_col + group_width], w_key[:, first_col:first_col + group_width].T, preferred_element_type=jnp.float32)
        term = term + jnp.dot(value_grad[:, first_col:first_col + group_width], w_value[:, first_col:first_col + group_width].T, preferred_element_type=jnp.float32)
        total_sum = total_sum + rounded(term)
    state_grad = total_sum.astype(jnp.bfloat16).reshape(NBRS, NL, D)
    return (context.reshape(TOKENS, HEADS * HEAD), query_grad.reshape(TOKENS, HEADS * HEAD), state_grad)
```

```python
import functools
import math

import jax
import jax.numpy as jnp
from jax import lax
from jax.experimental import pallas as pl
from jax.experimental.pallas import tpu as pltpu
from jax.sharding import PartitionSpec as P

HEAD = 128
CHUNKS = 2
GROUP = 2
F32 = jnp.float32
BF16 = jnp.bfloat16
NT = (((1,), (1,)), ((), ()))
TN = (((0,), (0,)), ((), ()))


def ring_order(chips):
    ny = 1 << ((chips.bit_length() - 1) // 2)
    nz = chips // ny
    order = [z * ny for z in range(nz)]
    for z in reversed(range(nz)):
        columns = range(1, ny) if (nz - 1 - z) % 2 == 0 else reversed(range(1, ny))
        order += [z * ny + y for y in columns]
    return order


class Ring:
    def __init__(self, chips):
        self.chips = chips
        self.order = ring_order(self.chips)
        self.position = [self.order.index(c) for c in range(self.chips)]
        n = self.chips
        pairs = [(self.order[q], self.order[(q + 1) % n]) for q in range(n)]
        self.up = pairs
        self.down = [(b, a) for a, b in pairs]

    def cw(self, x):
        return lax.ppermute(x, "chip", self.up)

    def ccw(self, x):
        return lax.ppermute(x, "chip", self.down)

    def other(self, x):
        return lax.ppermute(x, "core", [(0, 1), (1, 0)])

    def reach(self, flip):
        half = self.chips // 2
        return (half - 1, half) if flip else (half, half - 1)

    def gather(self, own, flip):
        n = self.chips
        ups, downs = self.reach(flip)
        out = [own] + [None] * (n - 1)
        up = down = own
        for s in range(1, max(ups, downs) + 1):
            if s <= ups:
                out[s] = up = self.cw(up)
            if s <= downs:
                out[n - s] = down = self.ccw(down)
        return out

    def reduce(self, part, flip):
        n = self.chips
        ups, downs = self.reach(flip)
        up = down = None

        def plus(a, b):
            return a if b is None else (a.astype(F32) + b.astype(F32)).astype(BF16)

        for s in range(max(ups, downs), 0, -1):
            if s <= ups:
                up = self.cw(plus(part[n - s], up))
            if s <= downs:
                down = self.ccw(plus(part[s], down))
        return part[0], up, down


def after(x, *others, cost=1):
    hbm = pl.BlockSpec(memory_space=pl.ANY)
    return pl.pallas_call(
        lambda *refs: None,
        out_shape=jax.ShapeDtypeStruct(x.shape, x.dtype),
        in_specs=[hbm] * (1 + len(others)),
        out_specs=hbm,
        input_output_aliases={0: 0},
        cost_estimate=pl.CostEstimate(flops=cost, bytes_accessed=1, transcendentals=0),
        name="after",
    )(x, *others)


def room(*shapes):
    return sum(math.prod(shape) * size for shape, size in shapes) + 8 * 1024 * 1024


def pieces(refs, depth):
    return [ref.at[pl.ds(i, depth)] for ref in refs for i in range(0, ref.shape[0], depth)]


def rows_kernel(count, depth, has_before, cuts, feature_ref, low_ref, high_ref, *refs):
    weights, refs = refs[:count], refs[count:]
    if has_before:
        before, refs = refs[0], refs[1:]
    outs, (held, sems) = refs[:cuts], refs[cuts:]
    views = pieces(weights, depth)
    copies = []
    for p, view in enumerate(views):
        copies.append(pltpu.make_async_copy(view, held.at[pl.ds(p * depth, depth)], sems.at[p]))
        copies[-1].start()
    wide = depth if depth % 128 == 0 else 2 * depth
    left = []
    for p in range(0, len(views), wide // depth):
        at = pl.ds(pl.multiple_of(feature_ref[p], wide), wide)
        left.append(jnp.concatenate([low_ref[:, at], high_ref[:, at]], axis=0))
    left = jnp.concatenate(left, axis=1)
    for copy in copies:
        copy.wait()
    total = jnp.dot(left, held[...], preferred_element_type=F32)
    if has_before:
        total += before[...]
    columns = outs[0].shape[1]
    for i, out in enumerate(outs):
        out[...] = total[:, i * columns : (i + 1) * columns].astype(out.dtype)


def add_rows(features, low, high, depth, weights, before, cuts):
    flat = [w for block in weights for w in block]
    tokens = low.shape[0]
    width = flat[0].shape[1]
    held = sum(w.shape[0] for w in flat)
    vmem = pl.BlockSpec(memory_space=pltpu.VMEM)
    earlier = [] if before is None else [before]
    outs = max(cuts, 1)
    out = jax.ShapeDtypeStruct((2 * tokens, width // outs), BF16 if cuts else F32)
    result = pl.pallas_call(
        functools.partial(rows_kernel, len(flat), depth, before is not None, outs),
        out_shape=[out] * outs,
        in_specs=[pl.BlockSpec(memory_space=pltpu.SMEM), vmem, vmem]
        + [pl.BlockSpec(memory_space=pl.ANY)] * len(flat)
        + [vmem] * len(earlier),
        out_specs=[vmem] * outs,
        scratch_shapes=[
            pltpu.VMEM((held, width), BF16),
            pltpu.SemaphoreType.DMA((held // depth,)),
        ],
        compiler_params=pltpu.CompilerParams(
            vmem_limit_bytes=room(
                (low.shape, 4), ((held, width), 2), ((2 * tokens, held), 2), ((2 * tokens, width), 12)
            )
        ),
        cost_estimate=pl.CostEstimate(
            flops=12 * tokens * held * width, bytes_accessed=2 * held * width, transcendentals=0
        ),
        name="rows",
    )(features, low, high, *flat, *earlier)
    return result if cuts else result[0]


PARTS = 4


def state_kernel(chunks, count, depth, dmodel, offset, info_ref, *refs):
    sums, weights, refs = refs[: 3 * chunks], refs[3 * chunks : 3 * chunks + count], refs[3 * chunks + count :]
    out_mine, out_pair, right, held, sems = refs
    tokens = right.shape[1] // 2
    features = held.shape[0]
    part = features // PARTS
    for p, view in enumerate(pieces(weights, depth)):
        to = lax.rem(info_ref[2 + p] - info_ref[0] + dmodel, dmodel) - offset

        @pl.when((to >= 0) & (to < features))
        def _(view=view, to=to):
            pltpu.make_async_copy(
                view, held.at[pl.ds(pl.multiple_of(to, depth), depth)], sems.at[lax.div(to, part)]
            ).start()

    width = sums[0].shape[1]
    for k in range(chunks):
        own, up, down = (sums[3 * k + j][...].astype(F32) for j in range(3))
        right[k * width : (k + 1) * width, :] = (own + up + down).astype(BF16).T
    second = info_ref[1] == 1
    for b in range(PARTS):
        at = slice(b * part, (b + 1) * part)
        block = held.at[pl.ds(b * part, part)]
        pltpu.make_async_copy(block, block, sems.at[b]).wait()
        total = jnp.dot(held[at, :], right[...], preferred_element_type=F32)
        low, high = total[:, :tokens], total[:, tokens:]
        out_mine[at, :] = jnp.where(second, high, low)
        out_pair[at, :] = jnp.where(second, low, high).astype(BF16)


def state_terms(info, offset, features, depth, dmodel, sums, weights):
    flat_sums = [x for group in sums for x in group]
    flat = [w for block in weights for w in block]
    tokens = flat_sums[0].shape[0]
    width = flat[0].shape[1]
    vmem, hbm = pl.BlockSpec(memory_space=pltpu.VMEM), pl.BlockSpec(memory_space=pl.ANY)
    return pl.pallas_call(
        functools.partial(state_kernel, len(sums), len(flat), depth, dmodel, offset),
        out_shape=[
            jax.ShapeDtypeStruct((features, tokens // 2), F32),
            jax.ShapeDtypeStruct((features, tokens // 2), BF16),
        ],
        in_specs=[pl.BlockSpec(memory_space=pltpu.SMEM)]
        + [vmem] * len(flat_sums)
        + [hbm] * len(flat),
        out_specs=[vmem, vmem],
        scratch_shapes=[
            pltpu.VMEM((width, tokens), BF16),
            pltpu.VMEM((features, width), BF16),
            pltpu.SemaphoreType.DMA((PARTS,)),
        ],
        compiler_params=pltpu.CompilerParams(
            vmem_limit_bytes=60 * 1024 * 1024
        ),
        cost_estimate=pl.CostEstimate(flops=1, bytes_accessed=1, transcendentals=0),
        name="state",
    )(info, *flat_sums, *flat)


def final_kernel(own_ref, got_ref, out_ref):
    out_ref[...] = (own_ref[...].astype(F32) + got_ref[...].astype(F32)).T.astype(BF16)


def finish(own, got):
    features, tokens = own.shape
    block = features // PARTS
    part = pl.BlockSpec((block, tokens), lambda i: (i, 0))
    return pl.pallas_call(
        final_kernel,
        out_shape=jax.ShapeDtypeStruct((tokens, features), BF16),
        grid=(PARTS,),
        in_specs=[part, part],
        out_specs=pl.BlockSpec((tokens, block), lambda i: (0, i)),
        compiler_params=pltpu.CompilerParams(vmem_limit_bytes=60 * 1024 * 1024),
        cost_estimate=pl.CostEstimate(
            flops=2 * own.size, bytes_accessed=6 * own.size, transcendentals=0
        ),
        name="finish",
    )(own, got)


def attend_kernel(blocks, heads, spans, neigh, offset, slot_ref, count_ref, *refs):
    tokens_hbm, rows_hbm, refs = refs[:4], refs[4 : 4 + blocks], refs[4 + blocks :]
    contexts, query_grads, grads = refs[0:2], refs[2:4], refs[4 : 4 + blocks]
    tokens, rows, total, sems = refs[4 + blocks :]
    width = heads * HEAD
    span_len = tokens.shape[1] // spans
    scale = 1.0 / math.sqrt(HEAD)
    length = rows.shape[1]
    copies = []
    for i, ref in enumerate(tokens_hbm):
        first = offset + (0 if i % 2 else slot_ref[slot_ref.shape[0] - 1])
        view = ref.at[:, pl.ds(pl.multiple_of(first, HEAD), width)]
        copies.append(pltpu.make_async_copy(view, tokens.at[i], sems.at[i]))
    for b in range(2 * blocks):
        view = rows_hbm[b // 2].at[pl.ds(b % 2 * length, length)]
        copies.append(pltpu.make_async_copy(view, rows.at[b], sems.at[4 + b]))
    for copy in copies:
        copy.start()
    queries, cotangents = [tokens.at[0], tokens.at[1]], [tokens.at[2], tokens.at[3]]
    total[...] = jnp.zeros_like(total)
    for copy in copies:
        copy.wait()

    def together(first, sides):
        chains = [
            (side, first + u, g) for u in range(GROUP) for side in sides for g in range(heads)
        ]
        at = [pl.ds(pl.multiple_of(span * span_len, span_len), span_len) for _, span, _ in chains]
        index = {
            (h, j): slot_ref[(side * spans + span) * neigh + j]
            for h, (side, span, _) in enumerate(chains)
            for j in range(neigh)
        }
        live = [
            [j < count_ref[side * spans + span] for j in range(neigh)] for side, span, _ in chains
        ]
        kcols = [slice(g * HEAD, (g + 1) * HEAD) for _, _, g in chains]
        vcols = [slice(width + g * HEAD, width + (g + 1) * HEAD) for _, _, g in chains]
        items = [(h, j) for h in range(len(chains)) for j in range(neigh)]
        query = [queries[chains[h][0]][at[h], c] for h, c in enumerate(kcols)]
        keys = {(h, j): rows[index[h, j], :, kcols[h]] for h, j in items}
        def diagonal(left, right, product, axis):
            out = {}
            for h in range(len(chains)):
                both = product(
                    jnp.concatenate([left[h, j] for j in range(neigh)]),
                    jnp.concatenate([right[h, j] for j in range(neigh)], axis=axis),
                    preferred_element_type=F32,
                )
                for j in range(neigh):
                    at = slice(j * span_len, (j + 1) * span_len)
                    out[h, j] = both[at, j * HEAD : (j + 1) * HEAD]
            return out

        length = rows.shape[1]
        joint = [jnp.concatenate([keys[h, j] for j in range(neigh)]) for h in range(len(chains))]
        joint = [
            lax.dot_general(query[h], joint[h], NT, preferred_element_type=F32)
            for h in range(len(chains))
        ]
        score = {(h, j): joint[h][:, j * length : (j + 1) * length] * scale for h, j in items}
        top = {i: jnp.max(score[i], axis=1, keepdims=True) for i in items}
        powers = {i: jnp.exp(score[i] - top[i]) for i in items}
        norm = {i: jnp.sum(powers[i], axis=1, keepdims=True) for i in items}
        prob = {i: powers[i] * (1.0 / norm[i]) for i in items}
        half = {i: prob[i].astype(BF16) for i in items}
        values = {(h, j): rows[index[h, j], :, vcols[h]] for h, j in items}
        part = {
            i: x.astype(BF16).astype(F32) for i, x in diagonal(half, values, jnp.dot, 1).items()
        }
        log_total = {i: top[i] + jnp.log(norm[i]) for i in items}
        mix, mixed = {}, {}
        for h in range(len(chains)):
            masked = [jnp.where(live[h][j], log_total[h, j], -1e30) for j in range(neigh)]
            best = functools.reduce(jnp.maximum, masked)
            raw = [jnp.where(live[h][j], jnp.exp(masked[j] - best), 0.0) for j in range(neigh)]
            below = 1.0 / functools.reduce(jnp.add, raw)
            for j in range(neigh):
                mix[h, j] = raw[j] * below
        cot = [cotangents[chains[h][0]][at[h], c].astype(F32) for h, c in enumerate(kcols)]
        exact = {(h, j): mix[h, j] * cot[h] for h, j in items}
        pgrad = {i: exact[i].astype(BF16) for i in items}
        dprob = diagonal(pgrad, values, functools.partial(lax.dot_general, dimension_numbers=NT), 0)
        for h in range(len(chains)):
            mixed[h] = functools.reduce(jnp.add, [mix[h, j] * part[h, j] for j in range(neigh)])
        rest_term = {
            (h, j): jnp.sum(
                (pgrad[h, j].astype(F32) - exact[h, j]) * part[h, j] + exact[h, j] * mixed[h],
                axis=1,
                keepdims=True,
            )
            for h, j in items
        }
        dscore = {i: (prob[i] * (dprob[i] - rest_term[i])).astype(BF16) for i in items}
        slot_dq = {
            i: (x * scale).astype(BF16).astype(F32)
            for i, x in diagonal(dscore, keys, jnp.dot, 1).items()
        }
        joint = [
            jnp.concatenate([dscore[h, j] for j in range(neigh)], axis=1)
            for h in range(len(chains))
        ]
        joint = [
            lax.dot_general(joint[h], query[h], TN, preferred_element_type=F32)
            for h in range(len(chains))
        ]
        dkey = {(h, j): joint[h][j * length : (j + 1) * length] for h, j in items}
        dvalue = {
            i: lax.dot_general(half[i], pgrad[i], TN, preferred_element_type=F32) for i in items
        }
        for h in range(len(chains)):
            contexts[chains[h][0]][at[h], kcols[h]] = mixed[h].astype(BF16)
            dquery = functools.reduce(jnp.add, [slot_dq[h, j] for j in range(neigh)])
            query_grads[chains[h][0]][at[h], kcols[h]] = dquery.astype(BF16)
        for h, j in items:
            total[index[h, j], :, kcols[h]] += dkey[h, j]
            total[index[h, j], :, vcols[h]] += dvalue[h, j]

    for sides in [(0, 1)] if heads <= 2 else [(0,), (1,)]:

        @pl.loop(0, spans // GROUP)
        def _(step):
            together(step * GROUP, sides)

    for b in range(rows.shape[0]):
        out, first = divmod(b * length, grads[0].shape[0])
        to = slice(first, first + length)
        grads[out][to, :width] = (total[b, :, :width] * scale).astype(BF16)
        grads[out][to, width:] = total[b, :, width:].astype(BF16)


def attend(slots, counts, tokens, rows, offset, spans, neigh):
    blocks = len(rows)
    count = tokens[0].shape[0]
    width = rows[0].shape[1] // 2
    heads = width // HEAD
    length = rows[0].shape[0] // 2
    span_len = count // spans
    vmem, hbm = pl.BlockSpec(memory_space=pltpu.VMEM), pl.BlockSpec(memory_space=pl.ANY)
    smem = pl.BlockSpec(memory_space=pltpu.SMEM)
    tok = jax.ShapeDtypeStruct((count, width), BF16)
    grad = jax.ShapeDtypeStruct((2 * length, 2 * width), BF16)
    work = 2 * spans * neigh * heads * span_len * length * HEAD * 2
    out = pl.pallas_call(
        functools.partial(attend_kernel, blocks, heads, spans, neigh, offset),
        out_shape=[tok] * 4 + [grad] * blocks,
        in_specs=[smem, smem] + [hbm] * (4 + blocks),
        out_specs=[vmem] * (4 + blocks),
        scratch_shapes=[
            pltpu.VMEM((4, count, width), BF16),
            pltpu.VMEM((2 * blocks, length, 2 * width), BF16),
            pltpu.VMEM((2 * blocks, length, 2 * width), F32),
            pltpu.SemaphoreType.DMA((4 + 2 * blocks,)),
        ],
        compiler_params=pltpu.CompilerParams(vmem_limit_bytes=60 * 1024 * 1024),
        cost_estimate=pl.CostEstimate(
            flops=20 * work,
            bytes_accessed=2 * blocks * length * width * 8,
            transcendentals=2 * spans * neigh * heads * span_len * length,
        ),
        name="attend",
    )(slots, counts, *tokens, *rows)
    return out[0:2], out[2:4], out[4:]


def columns_of(x, first, size):
    return lax.dynamic_slice_in_dim(x, first, size, axis=1)


def both_ways(core, mine, other):
    swapped = core == 1
    return jnp.concatenate([jnp.where(swapped, other, mine), jnp.where(swapped, mine, other)], axis=1)


def local(queries, neighbours, counts, states, w_key, w_value, cotangent):
    ring = Ring(lax.axis_size("chip"))
    chips = ring.chips
    chip, core = lax.axis_index("chip"), lax.axis_index("core")
    tensors, across = lax.axis_size("tensor"), lax.axis_index("tensor")
    place = jnp.asarray(ring.position, jnp.int32)
    here = place[chip]
    spans, neigh = neighbours.shape
    length, dmodel = states.shape[1:]
    half = queries.shape[1] // 2
    heads = half // HEAD
    chunks = min(CHUNKS, heads) if chips <= 8 else 1
    width = half // chunks
    first_mine, first_other = core * half, (1 - core) * half

    swapped = core == 1
    depth = w_key.shape[0]

    def in_order(mine, came):
        return jnp.where(swapped, came, mine), jnp.where(swapped, mine, came)

    keep, send = (
        jnp.concatenate(
            [
                columns_of(w, first + k * width, width)
                for k in range(chunks)
                for w in (w_key, w_value)
            ],
            axis=1,
        )
        for first in (first_mine, first_other)
    )
    shard = [keep, ring.other(send)]
    if depth % 128:
        shard = in_order(*shard)
    weights = [list(block) for block in zip(*(ring.gather(x, j) for j, x in enumerate(shard)))]
    mine_states = states.reshape(length, dmodel)
    low, high = in_order(mine_states, ring.other(mine_states))
    small = jnp.concatenate([neighbours, counts[:, None]], axis=1)
    small = jnp.stack([small, ring.other(small)])
    ids = small[:, :, :neigh].reshape(2 * spans * neigh)
    live_counts = small[:, :, neigh].reshape(2 * spans)
    slots = 2 * ((here - place[ids // 2]) % chips) + ids % 2
    behind = jnp.asarray(ring.order, jnp.int32)[(here - jnp.arange(chips, dtype=jnp.int32)) % chips]
    cores = jnp.arange(2, dtype=jnp.int32)
    if depth % 128 == 0:
        cores = cores ^ core
    features = (2 * behind[:, None] + cores[None, :]) * depth
    slots = jnp.concatenate([slots, first_mine[None]])
    tokens = [
        y for x in (queries, cotangent) for y in (x, ring.other(columns_of(x, first_other, half)))
    ]

    wide = dmodel // tensors
    info = jnp.concatenate([jnp.stack([(across + 1) % tensors * wide, core]), features.reshape(-1)])
    early = [r for r in range(chips) if min(r, chips - r) <= chips // 2 - 2]
    late = [r for r in range(chips) if r not in early]
    total = None
    for group in (early, late):
        where = jnp.stack([features[r] for r in group]).reshape(-1)
        picked = [weights[r] for r in group]
        total = add_rows(where, low, high, depth, picked, total, chunks if group is late else 0)
    context, query_grad, sums, rows = [], [], [], None
    for k in range(chunks):
        own = total[k]
        if k:
            ahead = min(2, chips // 2 - 1)
            own = after(own, rows[ahead], rows[chips - ahead])
        rows = ring.gather(own, k % 2)
        ctx, dq, parts = attend(slots, live_counts, tokens, rows, k * width, spans, neigh)
        context.append(ctx)
        query_grad.append(dq)
        sums.append(ring.reduce(parts, k % 2))
    swap_out = []
    for group in (context, query_grad):
        keep = jnp.concatenate([g[0] for g in group], axis=1)
        send = jnp.concatenate([g[1] for g in group], axis=1)
        swap_out.append(both_ways(core, keep, ring.other(send)))
    sums[0] = (after(sums[0][0], *swap_out),) + sums[0][1:]
    got = None
    for s in range(1, tensors + 1):
        ends = list(sums)
        if s > 1:
            ends[0] = (after(ends[0][0], term),) + tuple(ends[0][1:])
        term_mine, term_pair = state_terms(
            info, (s - 1) * wide, wide, depth, dmodel, ends, weights
        )
        term = (term_mine + ring.other(term_pair).astype(F32)).astype(BF16)
        if s < tensors:
            went = lax.ppermute(term, "tensor", [(i, (i + s) % tensors) for i in range(tensors)])
            got = went if got is None else got.astype(F32) + went.astype(F32)
    final = finish(term, after(got, cost=20_000_000_000))
    return swap_out[0], swap_out[1], final.reshape((1,) + final.shape)


def solution(mesh):
    devices = mesh.devices
    shape = (devices.shape[0] // 2, 2, devices.shape[1])
    by_chip = jax.sharding.Mesh(devices.reshape(shape), ("chip", "core", "tensor"))
    dp = ("chip", "core")
    placed = (
        P(dp, "tensor"),
        P(dp, None),
        P(dp),
        P(dp, None, None),
        P(dp, "tensor"),
        P(dp, "tensor"),
        P(dp, "tensor"),
    )
    return jax.shard_map(
        local,
        mesh=by_chip,
        in_specs=placed,
        out_specs=(P(dp, "tensor"), P(dp, "tensor"), P(dp, None, "tensor")),
        check_vma=False,
    )
```

```python
import functools
import math

import jax
import jax.numpy as jnp
from jax import lax
from jax.experimental import pallas as pl
from jax.experimental.pallas import tpu as pltpu
from jax.sharding import PartitionSpec as P

HEAD = 128
CHUNKS = 2
GROUP = 2
F32 = jnp.float32
BF16 = jnp.bfloat16
NT = (((1,), (1,)), ((), ()))
TN = (((0,), (0,)), ((), ()))


def ring_order(chips):
    ny = 1 << ((chips.bit_length() - 1) // 2)
    nz = chips // ny
    order = [z * ny for z in range(nz)]
    for z in reversed(range(nz)):
        columns = range(1, ny) if (nz - 1 - z) % 2 == 0 else reversed(range(1, ny))
        order += [z * ny + y for y in columns]
    return order


class Ring:
    def __init__(self, chips):
        self.chips = chips
        self.order = ring_order(self.chips)
        self.position = [self.order.index(c) for c in range(self.chips)]
        n = self.chips
        pairs = [(self.order[q], self.order[(q + 1) % n]) for q in range(n)]
        self.up = pairs
        self.down = [(b, a) for a, b in pairs]

    def cw(self, x):
        return lax.ppermute(x, "chip", self.up)

    def ccw(self, x):
        return lax.ppermute(x, "chip", self.down)

    def other(self, x):
        return lax.ppermute(x, "core", [(0, 1), (1, 0)])

    def reach(self, flip):
        half = self.chips // 2
        return (half - 1, half) if flip else (half, half - 1)

    def gather(self, own, flip):
        n = self.chips
        ups, downs = self.reach(flip)
        out = [own] + [None] * (n - 1)
        up = down = own
        for s in range(1, max(ups, downs) + 1):
            if s <= ups:
                out[s] = up = self.cw(up)
            if s <= downs:
                out[n - s] = down = self.ccw(down)
        return out

    def reduce(self, part, flip):
        n = self.chips
        ups, downs = self.reach(flip)
        up = down = None

        def plus(a, b):
            return a if b is None else (a.astype(F32) + b.astype(F32)).astype(BF16)

        for s in range(max(ups, downs), 0, -1):
            if s <= ups:
                up = self.cw(plus(part[n - s], up))
            if s <= downs:
                down = self.ccw(plus(part[s], down))
        return part[0], up, down


def after(x, *others, cost=1):
    hbm = pl.BlockSpec(memory_space=pl.ANY)
    return pl.pallas_call(
        lambda *refs: None,
        out_shape=jax.ShapeDtypeStruct(x.shape, x.dtype),
        in_specs=[hbm] * (1 + len(others)),
        out_specs=hbm,
        input_output_aliases={0: 0},
        cost_estimate=pl.CostEstimate(flops=cost, bytes_accessed=1, transcendentals=0),
        name="after",
    )(x, *others)


def room(*shapes):
    return sum(math.prod(shape) * size for shape, size in shapes) + 8 * 1024 * 1024


def pieces(refs, depth):
    return [ref.at[pl.ds(i, depth)] for ref in refs for i in range(0, ref.shape[0], depth)]


def rows_kernel(count, depth, has_before, cuts, feature_ref, low_ref, high_ref, *refs):
    weights, refs = refs[:count], refs[count:]
    if has_before:
        before, refs = refs[0], refs[1:]
    outs, (held, sems) = refs[:cuts], refs[cuts:]
    views = pieces(weights, depth)
    copies = []
    for p, view in enumerate(views):
        copies.append(pltpu.make_async_copy(view, held.at[pl.ds(p * depth, depth)], sems.at[p]))
        copies[-1].start()
    wide = depth if depth % 128 == 0 else 2 * depth
    left = []
    for p in range(0, len(views), wide // depth):
        at = pl.ds(pl.multiple_of(feature_ref[p], wide), wide)
        left.append(jnp.concatenate([low_ref[:, at], high_ref[:, at]], axis=0))
    left = jnp.concatenate(left, axis=1)
    for copy in copies:
        copy.wait()
    total = jnp.dot(left, held[...], preferred_element_type=F32)
    if has_before:
        total += before[...]
    columns = outs[0].shape[1]
    for i, out in enumerate(outs):
        out[...] = total[:, i * columns : (i + 1) * columns].astype(out.dtype)


def add_rows(features, low, high, depth, weights, before, cuts):
    flat = [w for block in weights for w in block]
    tokens = low.shape[0]
    width = flat[0].shape[1]
    held = sum(w.shape[0] for w in flat)
    vmem = pl.BlockSpec(memory_space=pltpu.VMEM)
    earlier = [] if before is None else [before]
    outs = max(cuts, 1)
    out = jax.ShapeDtypeStruct((2 * tokens, width // outs), BF16 if cuts else F32)
    result = pl.pallas_call(
        functools.partial(rows_kernel, len(flat), depth, before is not None, outs),
        out_shape=[out] * outs,
        in_specs=[pl.BlockSpec(memory_space=pltpu.SMEM), vmem, vmem]
        + [pl.BlockSpec(memory_space=pl.ANY)] * len(flat)
        + [vmem] * len(earlier),
        out_specs=[vmem] * outs,
        scratch_shapes=[
            pltpu.VMEM((held, width), BF16),
            pltpu.SemaphoreType.DMA((held // depth,)),
        ],
        compiler_params=pltpu.CompilerParams(
            vmem_limit_bytes=room(
                (low.shape, 4), ((held, width), 2), ((2 * tokens, held), 2), ((2 * tokens, width), 12)
            )
        ),
        cost_estimate=pl.CostEstimate(
            flops=12 * tokens * held * width, bytes_accessed=2 * held * width, transcendentals=0
        ),
        name="rows",
    )(features, low, high, *flat, *earlier)
    return result if cuts else result[0]


PARTS = 4


def state_kernel(chunks, count, depth, dmodel, offset, info_ref, *refs):
    sums, weights, refs = refs[: 3 * chunks], refs[3 * chunks : 3 * chunks + count], refs[3 * chunks + count :]
    out_mine, out_pair, right, held, terms, sems, term_sems = refs
    tokens = right.shape[1] // 2
    copies = [pltpu.make_async_copy(x, terms.at[i], term_sems.at[i]) for i, x in enumerate(sums)]
    for copy in copies:
        copy.start()
    features = held.shape[0]
    part = features // PARTS
    for p, view in enumerate(pieces(weights, depth)):
        to = lax.rem(info_ref[2 + p] - info_ref[0] + dmodel, dmodel) - offset

        @pl.when((to >= 0) & (to < features))
        def _(view=view, to=to):
            pltpu.make_async_copy(
                view, held.at[pl.ds(pl.multiple_of(to, depth), depth)], sems.at[lax.div(to, part)]
            ).start()

    width = sums[0].shape[1]
    for k in range(chunks):
        for copy in copies[3 * k : 3 * k + 3]:
            copy.wait()
        own, up, down = (terms[3 * k + j].astype(F32) for j in range(3))
        right[k * width : (k + 1) * width, :] = (own + up + down).astype(BF16).T
    second = info_ref[1] == 1
    for b in range(PARTS):
        at = slice(b * part, (b + 1) * part)
        block = held.at[pl.ds(b * part, part)]
        pltpu.make_async_copy(block, block, sems.at[b]).wait()
        total = jnp.dot(held[at, :], right[...], preferred_element_type=F32)
        low, high = total[:, :tokens], total[:, tokens:]
        out_mine[at, :] = jnp.where(second, high, low)
        out_pair[at, :] = jnp.where(second, low, high).astype(BF16)


def state_terms(info, offset, features, depth, dmodel, sums, weights):
    flat_sums = [x for group in sums for x in group]
    flat = [w for block in weights for w in block]
    tokens = flat_sums[0].shape[0]
    width = flat[0].shape[1]
    vmem, hbm = pl.BlockSpec(memory_space=pltpu.VMEM), pl.BlockSpec(memory_space=pl.ANY)
    return pl.pallas_call(
        functools.partial(state_kernel, len(sums), len(flat), depth, dmodel, offset),
        out_shape=[
            jax.ShapeDtypeStruct((features, tokens // 2), F32),
            jax.ShapeDtypeStruct((features, tokens // 2), BF16),
        ],
        in_specs=[pl.BlockSpec(memory_space=pltpu.SMEM)]
        + [hbm] * (len(flat_sums) + len(flat)),
        out_specs=[vmem, vmem],
        scratch_shapes=[
            pltpu.VMEM((width, tokens), BF16),
            pltpu.VMEM((features, width), BF16),
            pltpu.VMEM((len(flat_sums),) + flat_sums[0].shape, BF16),
            pltpu.SemaphoreType.DMA((PARTS,)),
            pltpu.SemaphoreType.DMA((len(flat_sums),)),
        ],
        compiler_params=pltpu.CompilerParams(
            vmem_limit_bytes=60 * 1024 * 1024
        ),
        cost_estimate=pl.CostEstimate(flops=1, bytes_accessed=1, transcendentals=0),
        name="state",
    )(info, *flat_sums, *flat)


def final_kernel(mine_ref, came_ref, got_ref, out_ref):
    term = (mine_ref[...] + came_ref[...].astype(F32)).astype(BF16)
    out_ref[...] = (term.astype(F32) + got_ref[...].astype(F32)).T.astype(BF16)


def finish(mine, came, got):
    vmem = pl.BlockSpec(memory_space=pltpu.VMEM)
    return pl.pallas_call(
        final_kernel,
        out_shape=jax.ShapeDtypeStruct(mine.shape[::-1], BF16),
        in_specs=[vmem, vmem, vmem],
        out_specs=vmem,
        compiler_params=pltpu.CompilerParams(vmem_limit_bytes=room((mine.shape, 28))),
        cost_estimate=pl.CostEstimate(
            flops=2 * mine.size, bytes_accessed=10 * mine.size, transcendentals=0
        ),
        name="finish",
    )(mine, came, got)


def attend_kernel(blocks, heads, spans, neigh, offset, slot_ref, count_ref, *refs):
    tokens_hbm, rows_hbm, refs = refs[:4], refs[4 : 4 + blocks], refs[4 + blocks :]
    contexts, query_grads, grads = refs[0:2], refs[2:4], refs[4 : 4 + blocks]
    tokens, rows, total, sems = refs[4 + blocks :]
    width = heads * HEAD
    span_len = tokens.shape[1] // spans
    scale = 1.0 / math.sqrt(HEAD)
    length = rows.shape[1]
    copies = []
    for i, ref in enumerate(tokens_hbm):
        first = offset + (0 if i % 2 else slot_ref[slot_ref.shape[0] - 1])
        view = ref.at[:, pl.ds(pl.multiple_of(first, HEAD), width)]
        copies.append(pltpu.make_async_copy(view, tokens.at[i], sems.at[i]))
    for b in range(2 * blocks):
        view = rows_hbm[b // 2].at[pl.ds(b % 2 * length, length)]
        copies.append(pltpu.make_async_copy(view, rows.at[b], sems.at[4 + b]))
    for copy in copies:
        copy.start()
    queries, cotangents = [tokens.at[0], tokens.at[1]], [tokens.at[2], tokens.at[3]]
    total[...] = jnp.zeros_like(total)
    for copy in copies:
        copy.wait()

    def together(first, sides):
        chains = [
            (side, first + u, g) for u in range(GROUP) for side in sides for g in range(heads)
        ]
        at = [pl.ds(pl.multiple_of(span * span_len, span_len), span_len) for _, span, _ in chains]
        index = {
            (h, j): slot_ref[(side * spans + span) * neigh + j]
            for h, (side, span, _) in enumerate(chains)
            for j in range(neigh)
        }
        live = [
            [j < count_ref[side * spans + span] for j in range(neigh)] for side, span, _ in chains
        ]
        kcols = [slice(g * HEAD, (g + 1) * HEAD) for _, _, g in chains]
        vcols = [slice(width + g * HEAD, width + (g + 1) * HEAD) for _, _, g in chains]
        items = [(h, j) for h in range(len(chains)) for j in range(neigh)]
        query = [queries[chains[h][0]][at[h], c] for h, c in enumerate(kcols)]
        keys = {(h, j): rows[index[h, j], :, kcols[h]] for h, j in items}
        def diagonal(left, right, product, axis):
            out = {}
            for h in range(len(chains)):
                both = product(
                    jnp.concatenate([left[h, j] for j in range(neigh)]),
                    jnp.concatenate([right[h, j] for j in range(neigh)], axis=axis),
                    preferred_element_type=F32,
                )
                columns = both.shape[1] // neigh
                for j in range(neigh):
                    at = slice(j * span_len, (j + 1) * span_len)
                    out[h, j] = both[at, j * columns : (j + 1) * columns]
            return out

        length = rows.shape[1]
        joint = [jnp.concatenate([keys[h, j] for j in range(neigh)]) for h in range(len(chains))]
        joint = [
            lax.dot_general(query[h], joint[h], NT, preferred_element_type=F32)
            for h in range(len(chains))
        ]
        score = {(h, j): joint[h][:, j * length : (j + 1) * length] * scale for h, j in items}
        top = {i: jnp.max(score[i], axis=1, keepdims=True) for i in items}
        powers = {i: jnp.exp(score[i] - top[i]) for i in items}
        norm = {i: jnp.sum(powers[i], axis=1, keepdims=True) for i in items}
        prob = {i: powers[i] * (1.0 / norm[i]) for i in items}
        half = {i: prob[i].astype(BF16) for i in items}
        values = {(h, j): rows[index[h, j], :, vcols[h]] for h, j in items}
        part = {
            i: x.astype(BF16).astype(F32) for i, x in diagonal(half, values, jnp.dot, 1).items()
        }
        log_total = {i: top[i] + jnp.log(norm[i]) for i in items}
        mix, mixed = {}, {}
        for h in range(len(chains)):
            masked = [jnp.where(live[h][j], log_total[h, j], -1e30) for j in range(neigh)]
            best = functools.reduce(jnp.maximum, masked)
            raw = [jnp.where(live[h][j], jnp.exp(masked[j] - best), 0.0) for j in range(neigh)]
            below = 1.0 / functools.reduce(jnp.add, raw)
            for j in range(neigh):
                mix[h, j] = raw[j] * below
        cot = [cotangents[chains[h][0]][at[h], c].astype(F32) for h, c in enumerate(kcols)]
        exact = {(h, j): mix[h, j] * cot[h] for h, j in items}
        pgrad = {i: exact[i].astype(BF16) for i in items}
        dprob = diagonal(pgrad, values, functools.partial(lax.dot_general, dimension_numbers=NT), 0)
        for h in range(len(chains)):
            mixed[h] = functools.reduce(jnp.add, [mix[h, j] * part[h, j] for j in range(neigh)])
        rest_term = {
            (h, j): jnp.sum(
                (pgrad[h, j].astype(F32) - exact[h, j]) * part[h, j] + exact[h, j] * mixed[h],
                axis=1,
                keepdims=True,
            )
            for h, j in items
        }
        dscore = {i: (prob[i] * (dprob[i] - rest_term[i])).astype(BF16) for i in items}
        slot_dq = {
            i: (x * scale).astype(BF16).astype(F32)
            for i, x in diagonal(dscore, keys, jnp.dot, 1).items()
        }
        joint = [
            jnp.concatenate([dscore[h, j] for j in range(neigh)], axis=1)
            for h in range(len(chains))
        ]
        joint = [
            lax.dot_general(joint[h], query[h], TN, preferred_element_type=F32)
            for h in range(len(chains))
        ]
        dkey = {(h, j): joint[h][j * length : (j + 1) * length] for h, j in items}
        dvalue = {
            i: lax.dot_general(half[i], pgrad[i], TN, preferred_element_type=F32) for i in items
        }
        for h in range(len(chains)):
            contexts[chains[h][0]][at[h], kcols[h]] = mixed[h].astype(BF16)
            dquery = functools.reduce(jnp.add, [slot_dq[h, j] for j in range(neigh)])
            query_grads[chains[h][0]][at[h], kcols[h]] = dquery.astype(BF16)
        for h, j in items:
            total[index[h, j], :, kcols[h]] += dkey[h, j]
            total[index[h, j], :, vcols[h]] += dvalue[h, j]

    for sides in [(0, 1)] if heads <= 2 else [(0,), (1,)]:

        @pl.loop(0, spans // GROUP)
        def _(step):
            together(step * GROUP, sides)

    for b in range(rows.shape[0]):
        out, first = divmod(b * length, grads[0].shape[0])
        to = slice(first, first + length)
        grads[out][to, :width] = (total[b, :, :width] * scale).astype(BF16)
        grads[out][to, width:] = total[b, :, width:].astype(BF16)


def attend(slots, counts, tokens, rows, offset, spans, neigh):
    blocks = len(rows)
    count = tokens[0].shape[0]
    width = rows[0].shape[1] // 2
    heads = width // HEAD
    length = rows[0].shape[0] // 2
    span_len = count // spans
    vmem, hbm = pl.BlockSpec(memory_space=pltpu.VMEM), pl.BlockSpec(memory_space=pl.ANY)
    smem = pl.BlockSpec(memory_space=pltpu.SMEM)
    tok = jax.ShapeDtypeStruct((count, width), BF16)
    grad = jax.ShapeDtypeStruct((2 * length, 2 * width), BF16)
    work = 2 * spans * neigh * heads * span_len * length * HEAD * 2
    out = pl.pallas_call(
        functools.partial(attend_kernel, blocks, heads, spans, neigh, offset),
        out_shape=[tok] * 4 + [grad] * blocks,
        in_specs=[smem, smem] + [hbm] * (4 + blocks),
        out_specs=[vmem] * (4 + blocks),
        scratch_shapes=[
            pltpu.VMEM((4, count, width), BF16),
            pltpu.VMEM((2 * blocks, length, 2 * width), BF16),
            pltpu.VMEM((2 * blocks, length, 2 * width), F32),
            pltpu.SemaphoreType.DMA((4 + 2 * blocks,)),
        ],
        compiler_params=pltpu.CompilerParams(vmem_limit_bytes=60 * 1024 * 1024),
        cost_estimate=pl.CostEstimate(
            flops=20 * work,
            bytes_accessed=2 * blocks * length * width * 8,
            transcendentals=2 * spans * neigh * heads * span_len * length,
        ),
        name="attend",
    )(slots, counts, *tokens, *rows)
    return out[0:2], out[2:4], out[4:]


def columns_of(x, first, size):
    return lax.dynamic_slice_in_dim(x, first, size, axis=1)


def both_ways(core, mine, other):
    swapped = core == 1
    return jnp.concatenate([jnp.where(swapped, other, mine), jnp.where(swapped, mine, other)], axis=1)


def local(queries, neighbours, counts, states, w_key, w_value, cotangent):
    ring = Ring(lax.axis_size("chip"))
    chips = ring.chips
    chip, core = lax.axis_index("chip"), lax.axis_index("core")
    tensors, across = lax.axis_size("tensor"), lax.axis_index("tensor")
    place = jnp.asarray(ring.position, jnp.int32)
    here = place[chip]
    spans, neigh = neighbours.shape
    length, dmodel = states.shape[1:]
    half = queries.shape[1] // 2
    heads = half // HEAD
    chunks = min(CHUNKS, heads) if chips <= 8 else 1
    width = half // chunks
    first_mine, first_other = core * half, (1 - core) * half

    swapped = core == 1
    depth = w_key.shape[0]

    def in_order(mine, came):
        return jnp.where(swapped, came, mine), jnp.where(swapped, mine, came)

    keep, send = (
        jnp.concatenate(
            [
                columns_of(w, first + k * width, width)
                for k in range(chunks)
                for w in (w_key, w_value)
            ],
            axis=1,
        )
        for first in (first_mine, first_other)
    )
    shard = [keep, ring.other(send)]
    if depth % 128:
        shard = in_order(*shard)
    weights = [list(block) for block in zip(*(ring.gather(x, j) for j, x in enumerate(shard)))]
    mine_states = states.reshape(length, dmodel)
    low, high = in_order(mine_states, ring.other(mine_states))
    small = jnp.concatenate([neighbours, counts[:, None]], axis=1)
    small = jnp.stack([small, ring.other(small)])
    ids = small[:, :, :neigh].reshape(2 * spans * neigh)
    live_counts = small[:, :, neigh].reshape(2 * spans)
    slots = 2 * ((here - place[ids // 2]) % chips) + ids % 2
    behind = jnp.asarray(ring.order, jnp.int32)[(here - jnp.arange(chips, dtype=jnp.int32)) % chips]
    cores = jnp.arange(2, dtype=jnp.int32)
    if depth % 128 == 0:
        cores = cores ^ core
    features = (2 * behind[:, None] + cores[None, :]) * depth
    slots = jnp.concatenate([slots, first_mine[None]])
    tokens = [
        y for x in (queries, cotangent) for y in (x, ring.other(columns_of(x, first_other, half)))
    ]

    wide = dmodel // tensors
    info = jnp.concatenate([jnp.stack([(across + 1) % tensors * wide, core]), features.reshape(-1)])
    early = [r for r in range(chips) if min(r, chips - r) <= chips // 2 - 2]
    late = [r for r in range(chips) if r not in early]
    total = None
    for group in (early, late):
        where = jnp.stack([features[r] for r in group]).reshape(-1)
        picked = [weights[r] for r in group]
        total = add_rows(where, low, high, depth, picked, total, chunks if group is late else 0)
    context, query_grad, sums, rows = [], [], [], None
    for k in range(chunks):
        own = total[k]
        if k:
            ahead = min(2, chips // 2 - 1)
            own = after(own, rows[ahead], rows[chips - ahead])
        rows = ring.gather(own, k % 2)
        ctx, dq, parts = attend(slots, live_counts, tokens, rows, k * width, spans, neigh)
        context.append(ctx)
        query_grad.append(dq)
        sums.append(ring.reduce(parts, k % 2))
    swap_out = []
    for group in (context, query_grad):
        keep = jnp.concatenate([g[0] for g in group], axis=1)
        send = jnp.concatenate([g[1] for g in group], axis=1)
        swap_out.append(both_ways(core, keep, ring.other(send)))
    sums[0] = (after(sums[0][0], *swap_out),) + sums[0][1:]
    got = None
    for s in range(1, tensors + 1):
        ends = list(sums)
        if s > 1:
            ends[0] = (after(ends[0][0], term),) + tuple(ends[0][1:])
        term_mine, term_pair = state_terms(
            info, (s - 1) * wide, wide, depth, dmodel, ends, weights
        )
        came = ring.other(term_pair)
        if s < tensors:
            term = (term_mine + came.astype(F32)).astype(BF16)
            went = lax.ppermute(term, "tensor", [(i, (i + s) % tensors) for i in range(tensors)])
            got = went if got is None else got.astype(F32) + went.astype(F32)
    final = finish(term_mine, came, after(got, cost=20_000_000_000))
    return swap_out[0], swap_out[1], final.reshape((1,) + final.shape)


def solution(mesh):
    devices = mesh.devices
    shape = (devices.shape[0] // 2, 2, devices.shape[1])
    by_chip = jax.sharding.Mesh(devices.reshape(shape), ("chip", "core", "tensor"))
    dp = ("chip", "core")
    placed = (
        P(dp, "tensor"),
        P(dp, None),
        P(dp),
        P(dp, None, None),
        P(dp, "tensor"),
        P(dp, "tensor"),
        P(dp, "tensor"),
    )
    return jax.shard_map(
        local,
        mesh=by_chip,
        in_specs=placed,
        out_specs=(P(dp, "tensor"), P(dp, "tensor"), P(dp, None, "tensor")),
        check_vma=False,
    )
```
